32 devices in a mesh: row: 4 (over y, x), col: 8 (over z, core).
Axes of the slice: x: 2, y: 2, z: 4, core: 2. Of those that a mesh axis runs over, the one named last changes fastest.
Arguments:
- density: bfloat16 [3072, 3072], P('row', 'col'), as said below
- pattern: int32 [2, 24, 24], P(None, 'row', 'col'), may hold values from 0 to 1, as said below
- kept_slots: int32 [2, 4, 8, 12], P(None, 'row', 'col'), may hold values from 0 to 17, as said below
- owner_shift: int32 [6], replicated, may hold values from 0 to 3
- owner_slot: int32 [4, 6], replicated, may hold values from 0 to 5, each once within a row
Outputs:
- purified: bfloat16 [3072, 3072], P('row', 'col')
- traces: float32 [2], replicated
The draws below stay inside these ranges and needn't reach their ends.
Inputs may be any that keep to these rules, and one draw needn't show every extreme that they name: Symmetric, as a density matrix is. `kept_slots`: each device's 12 entries of one multiply are distinct. `pattern`: symmetric in its last two dimensions; every diagonal block is 1. `owner_slot`: each row is a permutation.
All inputs are finite; a program needn't handle non-finite values.
Results may differ from the reference program's by a relative error of at most 0.0047.
Values may be sent and summed in bfloat16 or wider, within the bound.
A program may use at most 64 MiB of HBM per device.

```python
import math
import jax
import jax.numpy as jnp

BLOCK_DIM = 128
ROW_BLOCKS = 6
COL_BLOCKS = 3
KEPT = 12
ROW_GROUPS = 4
COL_GROUPS = 8
NBLOCKS = 24
ORDER = 3072


def draw_density(key, part):
    noise_key, diag_key = jax.random.split(jax.random.fold_in(key, 11))
    noise = jax.random.normal(noise_key, (ORDER, ORDER), jnp.float32)
    sym = (noise + noise.T) * (0.6 / math.sqrt(2.0 * ORDER))
    index = jnp.arange(ORDER)
    position = index.astype(jnp.float32) / (ORDER - 1.0)
    spread = jax.random.uniform(diag_key, (ORDER,), jnp.float32, 0.7, 1.3)
    diagonal = (0.25 + 0.5 * position) * spread
    return jnp.where(index[:, None] == index[None, :], diagonal[:, None], sym).astype(jnp.bfloat16)


def draw_pattern(key, part):
    values = jax.random.randint(jax.random.fold_in(key, 23), (2, NBLOCKS, NBLOCKS), 0, 10)
    upper = (values < 6).astype(jnp.int32)
    index = jnp.arange(NBLOCKS)
    above = (index[:, None] <= index[None, :])[None]
    sym = jnp.where(above, upper, jnp.swapaxes(upper, 1, 2))
    return jnp.where((index[:, None] == index[None, :])[None], 1, sym).astype(jnp.int32)


def draw_kept_slots(key, part):
    total = ROW_BLOCKS * COL_BLOCKS
    scores = jax.random.randint(jax.random.fold_in(key, 37), (2, ROW_GROUPS, COL_GROUPS, total), 0, 1 << 20)
    scores = scores * total + jnp.arange(total, dtype=jnp.int32)
    order = jnp.argsort(scores, axis=-1)
    return order[..., :KEPT].astype(jnp.int32)


def place_ends(entries, key, least, top_value):
    longest = entries.shape.index(max(entries.shape))
    spots = []
    for shift in (0, 1):
        where = [jax.random.randint(jax.random.fold_in(key, axis), (), 0, length) for axis, length in enumerate(entries.shape)]
        where[longest] = (where[longest] + shift) % entries.shape[longest]
        spots.append(tuple(where))
    return entries.at[spots[0]].set(least).at[spots[1]].set(top_value)


def setup_inputs(seed: int = 0) -> dict:
    arg_keys = jax.random.split(jax.random.key(seed), 6)
    return {
        "density": draw_density(jax.random.fold_in(arg_keys[5], 71), 0),
        "pattern": draw_pattern(jax.random.fold_in(arg_keys[5], 71), 0),
        "kept_slots": draw_kept_slots(jax.random.fold_in(arg_keys[5], 71), 0),
        "owner_shift": place_ends(jax.random.randint(arg_keys[3], (ROW_BLOCKS,), 0, ROW_GROUPS), jax.random.fold_in(arg_keys[3], 1), 0, ROW_GROUPS - 1).astype(jnp.int32),
        "owner_slot": jax.vmap(lambda own: jax.random.permutation(own, ROW_BLOCKS))(jax.random.split(arg_keys[4], ROW_GROUPS)).reshape((ROW_GROUPS, ROW_BLOCKS)).astype(jnp.int32),
    }


def expand(mask, size):
    return jnp.repeat(jnp.repeat(mask, size, axis=0), size, axis=1)


def kept_blocks(kept):
    slots = jnp.arange(ROW_BLOCKS * COL_BLOCKS, dtype=jnp.int32)
    hit = jnp.any(kept[..., None] == slots, axis=-2).astype(jnp.int32)
    hit = hit.reshape(ROW_GROUPS, COL_GROUPS, ROW_BLOCKS, COL_BLOCKS)
    return hit.transpose(0, 2, 1, 3).reshape(NBLOCKS, NBLOCKS)


def purify(current, occupancy, kept, flipped):
    operand = current * expand(occupancy, BLOCK_DIM).astype(current.dtype)
    square = jnp.dot(operand, operand, preferred_element_type=jnp.float32)
    if flipped:
        update = 2.0 * operand.astype(jnp.float32) - square
    else:
        update = square
    update = update * expand(kept_blocks(kept), BLOCK_DIM).astype(jnp.float32)
    return update.astype(jnp.bfloat16)


def reference(density, pattern, kept_slots, owner_shift, owner_slot):
    first = purify(density, pattern[0], kept_slots[0], False)
    trace_one = jnp.sum(jnp.diagonal(first.astype(jnp.float32)))
    blocks = jnp.arange(NBLOCKS, dtype=jnp.int32)
    groups = blocks // ROW_BLOCKS
    local = blocks % ROW_BLOCKS
    target_group = ((groups + owner_shift[local]) % ROW_GROUPS).astype(jnp.int32)
    target = target_group * ROW_BLOCKS + owner_slot[target_group, local]
    source = jnp.argsort(target).astype(jnp.int32)
    element = (source[:, None] * BLOCK_DIM + jnp.arange(BLOCK_DIM, dtype=jnp.int32)[None, :]).reshape(-1)
    relabelled = first[element][:, element]
    second = purify(relabelled, pattern[1], kept_slots[1], True)
    trace_two = jnp.sum(jnp.diagonal(second.astype(jnp.float32)))
    return second, jnp.stack([trace_one, trace_two])
```

```python
import jax
import jax.numpy as jnp
from jax import lax
from jax.sharding import PartitionSpec as P


def expand(mask, bdim, dtype):
    return jnp.repeat(jnp.repeat(mask, bdim, axis=0), bdim, axis=1).astype(dtype)


def product(left, right):
    steps, _, inner = left.shape
    right = right.reshape(steps, inner, right.shape[1])
    total = jnp.dot(left[0], right[0], preferred_element_type=jnp.float32)
    for step in range(1, steps):
        total = total + jnp.dot(left[step], right[step], preferred_element_type=jnp.float32)
    return total


def body(density, pattern, kept_slots, owner_shift, owner_slot):
    rows, cols = density.shape
    nrb, ncb = pattern.shape[1:]
    bdim = rows // nrb
    nrow, ncol = lax.axis_size("row"), lax.axis_size("col")
    nblocks = nrow * nrb
    row_index, col_index = lax.axis_index("row"), lax.axis_index("col")

    blocks = jnp.arange(nblocks, dtype=jnp.int32)
    local = blocks % nrb
    target_group = (blocks // nrb + owner_shift[local]) % nrow
    target = target_group * nrb + owner_slot[target_group, local]
    source = jnp.argsort(target).astype(jnp.int32)
    row_blocks = row_index * nrb + jnp.arange(nrb, dtype=jnp.int32)
    col_blocks = col_index * ncb + jnp.arange(ncb, dtype=jnp.int32)
    source_rows = source[row_blocks]
    source_cols = source[col_blocks]
    pattern_row = lax.all_gather(pattern[1], "col", axis=1, tiled=True)
    pattern_col = lax.all_gather(pattern[1], "row", axis=0, tiled=True)

    slots = jnp.arange(nrb * ncb, dtype=jnp.int32)
    keep = jnp.any(kept_slots[:, 0, 0, :, None] == slots, axis=1).reshape(2, nrb, ncb)

    operand = density * expand(pattern[0], bdim, density.dtype)
    left = lax.all_gather(operand, "col")
    right = lax.all_gather(operand, "row", axis=0, tiled=True)
    first = (product(left, right) * expand(keep[0], bdim, jnp.float32)).astype(jnp.bfloat16)

    by_row = lax.all_gather(first, "row", axis=0, tiled=True).reshape(nblocks, bdim, cols)
    by_col = lax.all_gather(first, "col")
    picked_rows = jnp.take(by_row, source_rows, axis=0).reshape(rows, cols)
    picked_rows = picked_rows * expand(pattern_row[:, target[col_blocks]], bdim, first.dtype)

    def pick(panels):
        return jnp.concatenate(
            [
                lax.dynamic_slice(
                    panels,
                    (source_cols[j] // ncb, 0, source_cols[j] % ncb * bdim),
                    (1, rows, bdim),
                )[0]
                for j in range(ncb)
            ],
            axis=1,
        )

    picked_cols = pick(by_col) * expand(pattern_col[target[row_blocks]], bdim, first.dtype)
    left = lax.all_gather(picked_rows, "col")
    right = lax.all_gather(picked_cols, "row", axis=0, tiled=True)
    square = product(left, right)
    update = 2.0 * pick(left).astype(jnp.float32) - square
    second = (update * expand(keep[1], bdim, jnp.float32)).astype(jnp.bfloat16)

    global_row = row_index * rows + jnp.arange(rows, dtype=jnp.int32)[:, None]
    global_col = col_index * cols + jnp.arange(cols, dtype=jnp.int32)[None, :]
    on_diagonal = global_row == global_col
    traces = jnp.stack(
        [jnp.sum(jnp.where(on_diagonal, t.astype(jnp.float32), 0.0)) for t in (first, second)]
    )
    return second, lax.psum(traces, ("row", "col"))


def solution(mesh):
    placed = (P("row", "col"), P(None, "row", "col"), P(None, "row", "col", None), P(), P())
    return jax.shard_map(
        body, mesh=mesh, in_specs=placed, out_specs=(P("row", "col"), P()), check_vma=False
    )
```

```python
import functools

import jax
import jax.numpy as jnp
from jax import lax
from jax.experimental import pallas as pl
from jax.experimental.pallas import tpu as pltpu
from jax.sharding import PartitionSpec as P

MESH = pl.DeviceIdType.MESH
F32 = jnp.float32
BF16 = jnp.bfloat16


def kernel(
    nrow, ncol, nrb, ncb, at,
    meta, dens, pat, out, traces,
    panel_0, panel_1, panel_2, column_0, column_1, column_2, pat_row, pat_col, sum_row, sum_col, acc, diag,
    p_recv, p_up, p_down, p_part, c_recv, c_send,
    pr_recv, pr_send, pc_recv, pc_send, sr_recv, sr_send, sc_recv, sc_send,
):
    panel, column = (panel_0, panel_1, panel_2), (column_0, column_1, column_2)
    rows, cols = dens.shape
    bdim = rows // nrb
    groups = ncol // 2
    r, c = lax.axis_index("row"), lax.axis_index("col")
    g, parity = c // 2, c % 2
    partner = 2 * g + 1 - parity

    def other_row(d):
        return lax.rem(r + d, nrow)

    def other_col(d):
        return lax.rem(c + d, ncol)

    barrier = pltpu.get_barrier_semaphore()
    for d in range(1, nrow):
        pl.semaphore_signal(barrier, inc=1, device_id=(other_row(d), c), device_id_type=MESH)
    for d in range(1, ncol):
        pl.semaphore_signal(barrier, inc=1, device_id=(r, other_col(d)), device_id_type=MESH)
    pl.semaphore_wait(barrier, nrow + ncol - 2)

    def remote(ref, send, recv, device):
        return pltpu.make_async_remote_copy(
            src_ref=ref, dst_ref=ref, send_sem=send, recv_sem=recv,
            device_id=device, device_id_type=MESH,
        )

    def along_col(ph, slot, to, sem):
        return remote(panel[ph].at[slot], sem.at[ph, slot], p_recv.at[ph, slot], (r, to))

    def along_row(ph, slot, to, d):
        return remote(column[ph].at[slot], c_send.at[ph, d], c_recv.at[ph, slot], (to, c))

    def small_row(buf, send, recv, slot, d):
        return remote(buf.at[slot], send.at[d], recv.at[slot], (other_row(d), c))

    def small_col(buf, send, recv, slot, d):
        return remote(buf.at[slot], send.at[d], recv.at[slot], (r, other_col(d)))

    def begin(ph):
        @pl.when(g + 1 < groups)
        def _():
            along_col(ph, c, c + 2, p_up).start()

        @pl.when(g > 0)
        def _():
            along_col(ph, c, c - 2, p_down).start()

        along_col(ph, c, partner, p_part).start()
        for d in range(1, nrow):
            along_row(ph, r, other_row(d), d).start()

    def relay(ph, d):
        below, above = g - d, g + d

        @pl.when(below >= 0)
        def _():
            slot = 2 * below + parity
            along_col(ph, slot, partner, p_part).wait_recv()

            @pl.when(g + 1 < groups)
            def _():
                along_col(ph, slot, c + 2, p_up).start()

            along_col(ph, slot, partner, p_part).start()

        @pl.when(above < groups)
        def _():
            slot = 2 * above + parity
            along_col(ph, slot, partner, p_part).wait_recv()

            @pl.when(g > 0)
            def _():
                along_col(ph, slot, c - 2, p_down).start()

            along_col(ph, slot, partner, p_part).start()

    def from_partner(ph, group):
        along_col(ph, 2 * group + 1 - parity, partner, p_part).wait_recv()

    def columns_in(ph):
        for d in range(1, nrow):
            along_row(ph, other_row(d), other_row(1), d).wait_recv()

    def finish(ph):
        along_col(ph, c, partner, p_part).wait_send()

        @pl.when(g + 1 < groups)
        def _():
            along_col(ph, c, c + 2, p_up).wait_send()

        @pl.when(g > 0)
        def _():
            along_col(ph, c, c - 2, p_down).wait_send()

        for d in range(1, groups):
            below, above = g - d, g + d

            @pl.when(below >= 0)
            def _():
                slot = 2 * below + parity

                @pl.when(g + 1 < groups)
                def _():
                    along_col(ph, slot, c + 2, p_up).wait_send()

                along_col(ph, slot, partner, p_part).wait_send()

            @pl.when(above < groups)
            def _():
                slot = 2 * above + parity

                @pl.when(g > 0)
                def _():
                    along_col(ph, slot, c - 2, p_down).wait_send()

                along_col(ph, slot, partner, p_part).wait_send()

        for d in range(1, nrow):
            along_row(ph, r, other_row(d), d).wait_send()

    half = rows // 2

    def compute(ph, d):
        def side(s, _):
            group = g + (2 * s - 1) * d

            @pl.when((group >= 0) & (group < groups) & ((d > 0) | (s > 0)))
            def _():
                from_partner(ph, group)

                def part(q, _):
                    right = column[ph][group, pl.ds(q * ncb, ncb)].reshape(cols, cols)
                    for k in range(2):
                        here = pl.ds(k * half, half)
                        left = jnp.concatenate(
                            [panel[ph][2 * group + q, j, here, :] for j in range(ncb)], axis=1
                        )
                        acc[here, :] += jnp.dot(left, right, preferred_element_type=F32)
                    return 0

                lax.fori_loop(0, 2, part, 0)

            return 0

        lax.fori_loop(0, 2, side, 0)

    def multiply(ph):
        acc[...] = jnp.zeros_like(acc)
        first = min(2, groups - 1)
        for d in range(1, groups):
            relay(ph, d)
            if d == first:
                columns_in(ph)

                def early(e, _):
                    compute(ph, e)
                    return 0

                lax.fori_loop(0, first + 1, early, 0)
            elif d > first:
                compute(ph, d)

    def block(i, j):
        return pl.ds(i * bdim, bdim), pl.ds(j * bdim, bdim)

    def trace_of(ref_value):
        total = jnp.zeros((bdim, bdim), F32)
        eye = lax.broadcasted_iota(jnp.int32, (bdim, bdim), 0) == lax.broadcasted_iota(
            jnp.int32, (bdim, bdim), 1
        )
        for i in range(nrb):
            for j in range(ncb):
                hit = r * nrb + i == c * ncb + j
                total += jnp.where(eye & hit, ref_value(i, j), 0.0)
        return jnp.sum(total, axis=0, keepdims=True)

    for i in range(nrb):
        for j in range(ncb):
            value = dens[block(i, j)] * meta[at["occupied"] + i * ncb + j].astype(F32).astype(BF16)
            panel[0][c, j, pl.ds(i * bdim, bdim), :] = value
            column[0][r, i, :, pl.ds(j * bdim, bdim)] = value
    begin(0)
    pat_row[c] = pat[...]
    pat_col[r] = pat[...]
    for d in range(1, nrow):
        small_row(pat_col, pc_send, pc_recv, r, d).start()
    for d in range(1, ncol):
        small_col(pat_row, pr_send, pr_recv, c, d).start()

    multiply(0)
    for i in range(nrb):
        for j in range(ncb):
            keep = meta[at["keep"] + i * ncb + j].astype(F32)
            value = (acc[block(i, j)] * keep).astype(BF16)
            panel[1][c, j, pl.ds(i * bdim, bdim), :] = value
            column[1][r, i, :, pl.ds(j * bdim, bdim)] = value
    begin(1)
    diag[...] = jnp.zeros_like(diag)
    diag[0:1, :] = trace_of(lambda i, j: panel[1][c, j, pl.ds(i * bdim, bdim), :].astype(F32))

    for d in range(1, ncol):
        small_col(pat_row, pr_send, pr_recv, other_col(d), 1).wait_recv()
    for d in range(1, nrow):
        small_row(pat_col, pc_send, pc_recv, other_row(d), 1).wait_recv()
    for d in range(1, groups):
        relay(1, d)
    columns_in(1)
    for i in range(nrb):
        for j in range(ncb):
            mask = pat_row[
                meta[at["col_to_dev"] + j], meta[at["col_to_local"] + j] * nrb + i
            ].astype(BF16)
            value = column[1][meta[at["row_dev"] + i], meta[at["row_local"] + i], :, pl.ds(j * bdim, bdim)
            ]
            panel[2][c, j, pl.ds(i * bdim, bdim), :] = value * mask

    def others(k, _):
        @pl.when(k != g)
        def _():
            from_partner(1, k)

        return 0

    from_partner(1, g)
    lax.fori_loop(0, groups, others, 0)
    for j in range(ncb):
        for i in range(nrb):
            mask = pat_col[
                meta[at["row_to_dev"] + i], meta[at["row_to_local"] + i] + nrb * j
            ].astype(BF16)
            value = panel[1][meta[at["col_dev"] + j], meta[at["col_local"] + j], pl.ds(i * bdim, bdim), :
            ]
            column[2][r, i, :, pl.ds(j * bdim, bdim)] = value * mask
    begin(2)
    multiply(2)
    for j in range(ncb):
        for i in range(nrb):
            keep = meta[at["keep"] + (nrb + i) * ncb + j].astype(F32)
            operand = panel[2][meta[at["col_dev"] + j], meta[at["col_local"] + j], pl.ds(i * bdim, bdim), :
            ]
            out[block(i, j)] = ((2.0 * operand.astype(F32) - acc[block(i, j)]) * keep).astype(BF16)
    diag[1:2, :] = trace_of(lambda i, j: out[block(i, j)].astype(F32))

    sum_row[r] = diag[...]
    for d in range(1, nrow):
        small_row(sum_row, sr_send, sr_recv, r, d).start()
    for ph in range(3):
        finish(ph)
    for d in range(1, nrow):
        small_row(sum_row, sr_send, sr_recv, other_row(d), 1).wait_recv()
    sum_col[c] = functools.reduce(lambda a, b: a + b, [sum_row[k] for k in range(nrow)])
    for d in range(1, ncol):
        small_col(sum_col, sc_send, sc_recv, c, d).start()
    for d in range(1, ncol):
        small_col(sum_col, sc_send, sc_recv, other_col(d), 1).wait_recv()
    total = functools.reduce(lambda a, b: a + b, [sum_col[k] for k in range(ncol)])
    traces[...] = jnp.broadcast_to(jnp.sum(total, axis=1, keepdims=True), traces.shape)
    for d in range(1, nrow):
        small_row(pat_col, pc_send, pc_recv, r, d).wait_send()
        small_row(sum_row, sr_send, sr_recv, r, d).wait_send()
    for d in range(1, ncol):
        small_col(pat_row, pr_send, pr_recv, c, d).wait_send()
        small_col(sum_col, sc_send, sc_recv, c, d).wait_send()


def body(density, pattern, kept_slots, owner_shift, owner_slot):
    rows, cols = density.shape
    nrb, ncb = pattern.shape[1:]
    nrow, ncol = lax.axis_size("row"), lax.axis_size("col")
    nblocks = nrow * nrb
    row_index, col_index = lax.axis_index("row"), lax.axis_index("col")

    blocks = jnp.arange(nblocks, dtype=jnp.int32)
    shift = jnp.tile(owner_shift, nrow)
    group_to = (blocks // nrb + shift) % nrow
    local = jnp.tile(jnp.arange(nrb, dtype=jnp.int32), nrow)
    slot_hit = (group_to[:, None, None] == jnp.arange(nrow)[None, :, None]) & (
        local[:, None, None] == jnp.arange(nrb)[None, None, :]
    )
    target = group_to * nrb + jnp.sum(jnp.where(slot_hit, owner_slot[None], 0), axis=(1, 2))
    row_blocks = row_index * nrb + jnp.arange(nrb, dtype=jnp.int32)
    col_blocks = col_index * ncb + jnp.arange(ncb, dtype=jnp.int32)

    def source_of(wanted):
        return jnp.sum(jnp.where(wanted[:, None] == target[None, :], blocks[None, :], 0), axis=1)

    source_rows, source_cols = source_of(row_blocks), source_of(col_blocks)
    target_rows = lax.dynamic_slice(target, (row_index * nrb,), (nrb,))
    target_cols = lax.dynamic_slice(target, (col_index * ncb,), (ncb,))
    slots = jnp.arange(nrb * ncb, dtype=jnp.int32)
    keep = jnp.any(kept_slots[:, 0, 0, :, None] == slots, axis=1)
    fields = {
        "row_dev": source_rows // nrb,
        "row_local": source_rows % nrb,
        "col_dev": source_cols // ncb,
        "col_local": source_cols % ncb,
        "row_to_dev": target_rows // nrb,
        "row_to_local": target_rows % nrb,
        "col_to_dev": target_cols // ncb,
        "col_to_local": target_cols % ncb,
        "occupied": pattern[0].reshape(-1),
        "keep": keep.reshape(-1).astype(jnp.int32),
    }
    at, offset = {}, 0
    for name, value in fields.items():
        at[name] = offset
        offset += value.size
    meta = jnp.concatenate([value.astype(jnp.int32) for value in fields.values()])
    small = jnp.broadcast_to(pattern[1].T.astype(F32).reshape(ncb * nrb, 1, 1), (ncb * nrb, 1, 128))

    dma = pltpu.SemaphoreType.DMA
    vmem = pl.BlockSpec(memory_space=pltpu.VMEM)
    scratch = [
        *[pltpu.VMEM((ncol, ncb, rows, rows // nrb), BF16)] * 3,
        *[pltpu.VMEM((nrow, nrb, rows // nrb, cols), BF16)] * 3,
        pltpu.VMEM((ncol, ncb * nrb, 1, 128), F32),
        pltpu.VMEM((nrow, ncb * nrb, 1, 128), F32),
        pltpu.VMEM((nrow, 8, 128), F32),
        pltpu.VMEM((ncol, 8, 128), F32),
        pltpu.VMEM((rows, cols), F32),
        pltpu.VMEM((8, 128), F32),
    ]
    held = 3 * (nrow + ncol) * rows * cols * 2
    second, sums = pl.pallas_call(
        functools.partial(kernel, nrow, ncol, nrb, ncb, at),
        out_shape=(
            jax.ShapeDtypeStruct((rows, cols), BF16),
            jax.ShapeDtypeStruct((8, 128), F32),
        ),
        in_specs=[pl.BlockSpec(memory_space=pltpu.SMEM), vmem, vmem],
        out_specs=(vmem, vmem),
        scratch_shapes=scratch
        + [dma((3, ncol))] * 4
        + [dma((3, nrow))] * 2
        + [dma((ncol,))] * 2
        + [dma((nrow,))] * 4
        + [dma((ncol,))] * 2,
        compiler_params=pltpu.CompilerParams(
            collective_id=0, has_side_effects=True, vmem_limit_bytes=held + (10 << 20)
        ),
        cost_estimate=pl.CostEstimate(
            flops=4 * rows * cols * nblocks * rows // nrb,
            bytes_accessed=4 * rows * cols,
            transcendentals=0,
        ),
    )(meta, density, small)
    return second, sums[:2, 0]


def solution(mesh):
    placed = (P("row", "col"), P(None, "row", "col"), P(None, "row", "col", None), P(), P())
    return jax.shard_map(
        body, mesh=mesh, in_specs=placed, out_specs=(P("row", "col"), P()), check_vma=False
    )
```

```python
import functools

import jax
import jax.numpy as jnp
from jax import lax
from jax.experimental import pallas as pl
from jax.experimental.pallas import tpu as pltpu
from jax.sharding import PartitionSpec as P

MESH = pl.DeviceIdType.MESH
F32 = jnp.float32
BF16 = jnp.bfloat16


def kernel(
    nrow, ncol, nrb, ncb, at,
    meta, dens, pat, out, traces,
    panel_0, panel_1, panel_2, column_0, column_1, column_2, pat_row, pat_col, sum_row, sum_col, acc, diag, served, given,
    p_recv, p_up, p_down, p_part, c_recv, c_send,
    pr_recv, pr_send, pc_recv, pc_send, sr_recv, sr_send, sc_recv, sc_send, give_recv, give_send,
):
    panel, column = (panel_0, panel_1, panel_2), (column_0, column_1, column_2)
    rows, cols = dens.shape
    bdim = rows // nrb
    groups = ncol // 2
    r, c = lax.axis_index("row"), lax.axis_index("col")
    g, parity = c // 2, c % 2
    partner = 2 * g + 1 - parity

    def other_row(d):
        return lax.rem(r + d, nrow)

    def other_col(d):
        return lax.rem(c + d, ncol)

    barrier = pltpu.get_barrier_semaphore()
    for d in range(1, nrow):
        pl.semaphore_signal(barrier, inc=1, device_id=(other_row(d), c), device_id_type=MESH)
    for d in range(1, ncol):
        pl.semaphore_signal(barrier, inc=1, device_id=(r, other_col(d)), device_id_type=MESH)
    pl.semaphore_wait(barrier, nrow + ncol - 2)

    def remote(ref, send, recv, device):
        return pltpu.make_async_remote_copy(
            src_ref=ref, dst_ref=ref, send_sem=send, recv_sem=recv,
            device_id=device, device_id_type=MESH,
        )

    def along_col(ph, slot, to, sem):
        return remote(panel[ph].at[slot], sem.at[ph, slot], p_recv.at[ph, slot], (r, to))

    def along_row(ph, slot, to, d):
        return remote(column[ph].at[slot], c_send.at[ph, d], c_recv.at[ph, slot], (to, c))

    def small_row(buf, send, recv, slot, d):
        return remote(buf.at[slot], send.at[d], recv.at[slot], (other_row(d), c))

    def small_col(buf, send, recv, slot, d):
        return remote(buf.at[slot], send.at[d], recv.at[slot], (r, other_col(d)))

    inner = (g > 0) & (g + 1 < groups)

    def lanes(ph):
        end = 1 if ph == 1 else 0
        return g + 1 < groups - end, g > end, inner if ph == 1 else g >= 0

    def hand_on(ph, slot, up, down, act):
        if up is not None:
            @pl.when(up)
            def _():
                act(along_col(ph, slot, c + 2, p_up))

        if down is not None:
            @pl.when(down)
            def _():
                act(along_col(ph, slot, c - 2, p_down))

    def start(copy):
        copy.start()

    def sent(copy):
        copy.wait_send()

    def begin_col(ph):
        up, down, any_in = lanes(ph)
        hand_on(ph, c, up, down, start)

        @pl.when(any_in)
        def _():
            along_col(ph, c, partner, p_part).start()

    def begin_row(ph):
        for d in range(1, nrow):
            along_row(ph, r, other_row(d), d).start()

    def relayed(ph, d, act, incoming):
        up, down, any_in = lanes(ph)
        for group, inside, to_up, to_down in (
            (g - d, g - d >= 0, up, None),
            (g + d, g + d < groups, None, down),
        ):
            @pl.when(inside & any_in)
            def _():
                slot = 2 * group + parity
                if incoming:
                    along_col(ph, slot, partner, p_part).wait_recv()
                hand_on(ph, slot, to_up, to_down, act)
                act(along_col(ph, slot, partner, p_part))

    def relay(ph, d):
        relayed(ph, d, start, True)

    def from_partner(ph, group):
        along_col(ph, 2 * group + 1 - parity, partner, p_part).wait_recv()

    def columns_in(ph):
        for d in range(1, nrow):
            along_row(ph, other_row(d), other_row(1), d).wait_recv()

    def finish(ph):
        up, down, any_in = lanes(ph)
        hand_on(ph, c, up, down, sent)

        @pl.when(any_in)
        def _():
            along_col(ph, c, partner, p_part).wait_send()

        for d in range(1, groups):
            relayed(ph, d, sent, False)
        for d in range(1, nrow):
            along_row(ph, r, other_row(d), d).wait_send()

    def serve(act):
        @pl.when(g == groups - 2)
        def _():
            act(give(c + 2))

        @pl.when(g == 1)
        def _():
            act(give(c - 2))

    def give(to):
        return pltpu.make_async_remote_copy(
            src_ref=served, dst_ref=given, send_sem=give_send.at[0], recv_sem=give_recv.at[0],
            device_id=(r, to), device_id_type=MESH,
        )

    half = rows // 2

    def compute(ph, d):
        def side(s, _):
            group = g + (2 * s - 1) * d

            @pl.when((group >= 0) & (group < groups) & ((d > 0) | (s > 0)))
            def _():
                from_partner(ph, group)

                def part(q, _):
                    right = column[ph][group, pl.ds(q * ncb, ncb)].reshape(cols, cols)
                    for k in range(2):
                        here = pl.ds(k * half, half)
                        left = jnp.concatenate(
                            [panel[ph][2 * group + q, j, here, :] for j in range(ncb)], axis=1
                        )
                        acc[here, :] += jnp.dot(left, right, preferred_element_type=F32)
                    return 0

                lax.fori_loop(0, 2, part, 0)

            return 0

        lax.fori_loop(0, 2, side, 0)

    def multiply(ph):
        acc[...] = jnp.zeros_like(acc)
        first = min(2, groups - 1)
        for d in range(1, groups):
            relay(ph, d)
            if d == first:
                columns_in(ph)

                def early(e, _):
                    compute(ph, e)
                    return 0

                lax.fori_loop(0, first + 1, early, 0)
            elif d > first:
                compute(ph, d)

    def block(i, j):
        return pl.ds(i * bdim, bdim), pl.ds(j * bdim, bdim)

    def trace_of(ref_value):
        total = jnp.zeros((bdim, bdim), F32)
        eye = lax.broadcasted_iota(jnp.int32, (bdim, bdim), 0) == lax.broadcasted_iota(
            jnp.int32, (bdim, bdim), 1
        )
        for i in range(nrb):
            for j in range(ncb):
                hit = r * nrb + i == c * ncb + j
                total += jnp.where(eye & hit, ref_value(i, j), 0.0)
        return jnp.sum(total, axis=0, keepdims=True)

    for i in range(nrb):
        for j in range(ncb):
            value = dens[block(i, j)] * meta[at["occupied"] + i * ncb + j].astype(F32).astype(BF16)
            panel[0][c, j, pl.ds(i * bdim, bdim), :] = value
            column[0][r, i, :, pl.ds(j * bdim, bdim)] = value
    begin_col(0)
    begin_row(0)
    pat_row[c] = pat[...]
    pat_col[r] = pat[...]
    for d in range(1, nrow):
        small_row(pat_col, pc_send, pc_recv, r, d).start()
    for d in range(1, ncol):
        small_col(pat_row, pr_send, pr_recv, c, d).start()

    multiply(0)
    for i in range(nrb):
        for j in range(ncb):
            keep = meta[at["keep"] + i * ncb + j].astype(F32)
            value = (acc[block(i, j)] * keep).astype(BF16)
            panel[1][c, j, pl.ds(i * bdim, bdim), :] = value
            column[1][r, i, :, pl.ds(j * bdim, bdim)] = value
    begin_row(1)
    begin_col(1)
    diag[...] = jnp.zeros_like(diag)
    diag[0:1, :] = trace_of(lambda i, j: panel[1][c, j, pl.ds(i * bdim, bdim), :].astype(F32))

    for d in range(1, ncol):
        small_col(pat_row, pr_send, pr_recv, other_col(d), 1).wait_recv()
    for d in range(1, nrow):
        small_row(pat_col, pc_send, pc_recv, other_row(d), 1).wait_recv()
    relay(1, 1)
    columns_in(1)
    for i in range(nrb):
        for j in range(ncb):
            mask = pat_row[
                meta[at["col_to_dev"] + j], meta[at["col_to_local"] + j] * nrb + i
            ].astype(BF16)
            value = column[1][meta[at["row_dev"] + i], meta[at["row_local"] + i], :, pl.ds(j * bdim, bdim)
            ]
            panel[2][c, j, pl.ds(i * bdim, bdim), :] = value * mask

    begin_col(2)
    for d in range(2, groups):
        relay(1, d)

    @pl.when(inner)
    def _():
        def arrived(k, _):
            from_partner(1, k)
            return 0

        lax.fori_loop(0, groups, arrived, 0)

        @pl.when((g == groups - 2) | (g == 1))
        def _():
            for j in range(ncb):
                served[j] = panel[1][meta[at["serve_dev"] + j], meta[at["serve_local"] + j]]

        serve(start)
        for j in range(ncb):
            given[j] = panel[1][meta[at["col_dev"] + j], meta[at["col_local"] + j]]

    @pl.when(jnp.logical_not(inner))
    def _():
        give(partner).wait_recv()

    for j in range(ncb):
        for i in range(nrb):
            mask = pat_col[
                meta[at["row_to_dev"] + i], meta[at["row_to_local"] + i] + nrb * j
            ].astype(BF16)
            value = given[j, pl.ds(i * bdim, bdim), :]
            column[2][r, i, :, pl.ds(j * bdim, bdim)] = value * mask
    begin_row(2)
    multiply(2)
    for j in range(ncb):
        for i in range(nrb):
            keep = meta[at["keep"] + (nrb + i) * ncb + j].astype(F32)
            operand = panel[2][meta[at["col_dev"] + j], meta[at["col_local"] + j], pl.ds(i * bdim, bdim), :
            ]
            out[block(i, j)] = ((2.0 * operand.astype(F32) - acc[block(i, j)]) * keep).astype(BF16)
    diag[1:2, :] = trace_of(lambda i, j: out[block(i, j)].astype(F32))

    sum_row[r] = diag[...]
    for d in range(1, nrow):
        small_row(sum_row, sr_send, sr_recv, r, d).start()
    for ph in range(3):
        finish(ph)
    serve(sent)
    for d in range(1, nrow):
        small_row(sum_row, sr_send, sr_recv, other_row(d), 1).wait_recv()
    sum_col[c] = functools.reduce(lambda a, b: a + b, [sum_row[k] for k in range(nrow)])
    for d in range(1, ncol):
        small_col(sum_col, sc_send, sc_recv, c, d).start()
    for d in range(1, ncol):
        small_col(sum_col, sc_send, sc_recv, other_col(d), 1).wait_recv()
    total = functools.reduce(lambda a, b: a + b, [sum_col[k] for k in range(ncol)])
    traces[...] = jnp.broadcast_to(jnp.sum(total, axis=1, keepdims=True), traces.shape)
    for d in range(1, nrow):
        small_row(pat_col, pc_send, pc_recv, r, d).wait_send()
        small_row(sum_row, sr_send, sr_recv, r, d).wait_send()
    for d in range(1, ncol):
        small_col(pat_row, pr_send, pr_recv, c, d).wait_send()
        small_col(sum_col, sc_send, sc_recv, c, d).wait_send()


def body(density, pattern, kept_slots, owner_shift, owner_slot):
    rows, cols = density.shape
    nrb, ncb = pattern.shape[1:]
    nrow, ncol = lax.axis_size("row"), lax.axis_size("col")
    nblocks = nrow * nrb
    row_index, col_index = lax.axis_index("row"), lax.axis_index("col")

    blocks = jnp.arange(nblocks, dtype=jnp.int32)
    shift = jnp.tile(owner_shift, nrow)
    group_to = (blocks // nrb + shift) % nrow
    local = jnp.tile(jnp.arange(nrb, dtype=jnp.int32), nrow)
    slot_hit = (group_to[:, None, None] == jnp.arange(nrow)[None, :, None]) & (
        local[:, None, None] == jnp.arange(nrb)[None, None, :]
    )
    target = group_to * nrb + jnp.sum(jnp.where(slot_hit, owner_slot[None], 0), axis=(1, 2))
    row_blocks = row_index * nrb + jnp.arange(nrb, dtype=jnp.int32)
    col_blocks = col_index * ncb + jnp.arange(ncb, dtype=jnp.int32)

    def source_of(wanted):
        return jnp.sum(jnp.where(wanted[:, None] == target[None, :], blocks[None, :], 0), axis=1)

    source_rows, source_cols = source_of(row_blocks), source_of(col_blocks)
    serve_col = jnp.where(col_index // 2 == 1, col_index - 2, lax.rem(col_index + 2, ncol))
    served_cols = source_of(serve_col * ncb + jnp.arange(ncb, dtype=jnp.int32))
    target_rows = lax.dynamic_slice(target, (row_index * nrb,), (nrb,))
    target_cols = lax.dynamic_slice(target, (col_index * ncb,), (ncb,))
    slots = jnp.arange(nrb * ncb, dtype=jnp.int32)
    keep = jnp.any(kept_slots[:, 0, 0, :, None] == slots, axis=1)
    fields = {
        "row_dev": source_rows // nrb,
        "row_local": source_rows % nrb,
        "col_dev": source_cols // ncb,
        "col_local": source_cols % ncb,
        "serve_dev": served_cols // ncb,
        "serve_local": served_cols % ncb,
        "row_to_dev": target_rows // nrb,
        "row_to_local": target_rows % nrb,
        "col_to_dev": target_cols // ncb,
        "col_to_local": target_cols % ncb,
        "occupied": pattern[0].reshape(-1),
        "keep": keep.reshape(-1).astype(jnp.int32),
    }
    at, offset = {}, 0
    for name, value in fields.items():
        at[name] = offset
        offset += value.size
    meta = jnp.concatenate([value.astype(jnp.int32) for value in fields.values()])
    small = jnp.broadcast_to(pattern[1].T.astype(F32).reshape(ncb * nrb, 1, 1), (ncb * nrb, 1, 128))

    dma = pltpu.SemaphoreType.DMA
    vmem = pl.BlockSpec(memory_space=pltpu.VMEM)
    scratch = [
        *[pltpu.VMEM((ncol, ncb, rows, rows // nrb), BF16)] * 3,
        *[pltpu.VMEM((nrow, nrb, rows // nrb, cols), BF16)] * 3,
        pltpu.VMEM((ncol, ncb * nrb, 1, 128), F32),
        pltpu.VMEM((nrow, ncb * nrb, 1, 128), F32),
        pltpu.VMEM((nrow, 8, 128), F32),
        pltpu.VMEM((ncol, 8, 128), F32),
        pltpu.VMEM((rows, cols), F32),
        pltpu.VMEM((8, 128), F32),
        *[pltpu.VMEM((ncb, rows, rows // nrb), BF16)] * 2,
    ]
    held = 3 * (nrow + ncol) * rows * cols * 2
    second, sums = pl.pallas_call(
        functools.partial(kernel, nrow, ncol, nrb, ncb, at),
        out_shape=(
            jax.ShapeDtypeStruct((rows, cols), BF16),
            jax.ShapeDtypeStruct((8, 128), F32),
        ),
        in_specs=[pl.BlockSpec(memory_space=pltpu.SMEM), vmem, vmem],
        out_specs=(vmem, vmem),
        scratch_shapes=scratch
        + [dma((3, ncol))] * 4
        + [dma((3, nrow))] * 2
        + [dma((ncol,))] * 2
        + [dma((nrow,))] * 4
        + [dma((ncol,))] * 2
        + [dma((1,))] * 2,
        compiler_params=pltpu.CompilerParams(
            collective_id=0, has_side_effects=True, vmem_limit_bytes=held + (10 << 20)
        ),
        cost_estimate=pl.CostEstimate(
            flops=4 * rows * cols * nblocks * rows // nrb,
            bytes_accessed=4 * rows * cols,
            transcendentals=0,
        ),
    )(meta, density, small)
    return second, sums[:2, 0]


def solution(mesh):
    placed = (P("row", "col"), P(None, "row", "col"), P(None, "row", "col", None), P(), P())
    return jax.shard_map(
        body, mesh=mesh, in_specs=placed, out_specs=(P("row", "col"), P()), check_vma=False
    )
```

```python
import functools

import jax
import jax.numpy as jnp
from jax import lax
from jax.experimental import pallas as pl
from jax.experimental.pallas import tpu as pltpu
from jax.sharding import PartitionSpec as P

MESH = pl.DeviceIdType.MESH
F32 = jnp.float32
BF16 = jnp.bfloat16


def kernel(
    nrow, ncol, nrb, ncb, at,
    meta, dens, pat, out, traces,
    panel_0, panel_1, panel_2, *rest,
):
    panel = (panel_0, panel_1, panel_2)
    column = [rest[ph * ncb : (ph + 1) * ncb] for ph in range(3)]
    (
        pat_row, pat_col, sum_row, sum_col, acc, diag, served, given,
        p_recv, p_up, p_down, p_part, c_recv, c_send,
        pr_recv, pr_send, pc_recv, pc_send, sr_recv, sr_send, sc_recv, sc_send,
        give_recv, give_send,
    ) = rest[3 * ncb :]
    rows, cols = dens.shape
    bdim = rows // nrb
    groups = ncol // 2
    r, c = lax.axis_index("row"), lax.axis_index("col")
    g, parity = c // 2, c % 2
    partner = 2 * g + 1 - parity

    def other_row(d):
        return lax.rem(r + d, nrow)

    def other_col(d):
        return lax.rem(c + d, ncol)

    barrier = pltpu.get_barrier_semaphore()
    for d in range(1, nrow):
        pl.semaphore_signal(barrier, inc=1, device_id=(other_row(d), c), device_id_type=MESH)
    for d in range(1, ncol):
        pl.semaphore_signal(barrier, inc=1, device_id=(r, other_col(d)), device_id_type=MESH)
    pl.semaphore_wait(barrier, nrow + ncol - 2)

    def remote(ref, send, recv, device):
        return pltpu.make_async_remote_copy(
            src_ref=ref, dst_ref=ref, send_sem=send, recv_sem=recv,
            device_id=device, device_id_type=MESH,
        )

    def along_col(ph, slot, j, to, sem):
        return remote(panel[ph].at[slot, j], sem.at[ph, slot, j], p_recv.at[ph, slot, j], (r, to))

    def along_row(ph, slot, j, to, d):
        return remote(column[ph][j].at[slot], c_send.at[ph, d, j], c_recv.at[ph, slot, j], (to, c))

    def small_row(buf, send, recv, slot, d):
        return remote(buf.at[slot], send.at[d], recv.at[slot], (other_row(d), c))

    def small_col(buf, send, recv, slot, d):
        return remote(buf.at[slot], send.at[d], recv.at[slot], (r, other_col(d)))

    inner = (g > 0) & (g + 1 < groups)

    def lanes(ph):
        end = 1 if ph == 1 else 0
        return g + 1 < groups - end, g > end, inner if ph == 1 else g >= 0

    def hand_on(ph, slot, j, up, down, act):
        if up is not None:
            @pl.when(up)
            def _():
                act(along_col(ph, slot, j, c + 2, p_up))

        if down is not None:
            @pl.when(down)
            def _():
                act(along_col(ph, slot, j, c - 2, p_down))

    def start(copy):
        copy.start()

    def sent(copy):
        copy.wait_send()

    def own_col(ph, j, act):
        up, down, any_in = lanes(ph)
        hand_on(ph, c, j, up, down, act)

        @pl.when(any_in)
        def _():
            act(along_col(ph, c, j, partner, p_part))

    def own_row(ph, j, act):
        for d in range(1, nrow):
            act(along_row(ph, r, j, other_row(d), d))

    def relayed(ph, d, j, act, incoming):
        up, down, any_in = lanes(ph)
        for group, inside, to_up, to_down in (
            (g - d, g - d >= 0, up, None),
            (g + d, g + d < groups, None, down),
        ):
            @pl.when(inside & any_in)
            def _():
                slot = 2 * group + parity
                if incoming:
                    along_col(ph, slot, j, partner, p_part).wait_recv()
                hand_on(ph, slot, j, to_up, to_down, act)
                act(along_col(ph, slot, j, partner, p_part))

    def relay(ph, d):
        for j in range(ncb):
            relayed(ph, d, j, start, True)

    def from_partner(ph, group):
        for j in range(ncb):
            along_col(ph, 2 * group + 1 - parity, j, partner, p_part).wait_recv()

    def columns_in(ph, j):
        for d in range(1, nrow):
            along_row(ph, other_row(d), j, other_row(1), d).wait_recv()

    def finish(ph):
        for j in range(ncb):
            own_col(ph, j, sent)
            own_row(ph, j, sent)
            for d in range(1, groups):
                relayed(ph, d, j, sent, False)

    def serve(j, act):
        @pl.when(g == groups - 2)
        def _():
            act(give(j, c + 2))

        @pl.when(g == 1)
        def _():
            act(give(j, c - 2))

    def give(j, to):
        return pltpu.make_async_remote_copy(
            src_ref=served.at[j], dst_ref=given.at[j],
            send_sem=give_send.at[j], recv_sem=give_recv.at[j],
            device_id=(r, to), device_id_type=MESH,
        )

    half = rows // 2

    def compute(ph, d):
        def side(s, _):
            group = g + (2 * s - 1) * d

            @pl.when((group >= 0) & (group < groups) & ((d > 0) | (s > 0)))
            def _():
                from_partner(ph, group)

                def part(q, _):
                    right = jnp.concatenate(
                        [column[ph][j][group, pl.ds(q * ncb, ncb)].reshape(cols, bdim) for j in range(ncb)],
                        axis=1,
                    )
                    for k in range(2):
                        here = pl.ds(k * half, half)
                        left = jnp.concatenate(
                            [panel[ph][2 * group + q, j, here, :] for j in range(ncb)], axis=1
                        )
                        acc[here, :] += jnp.dot(left, right, preferred_element_type=F32)
                    return 0

                lax.fori_loop(0, 2, part, 0)

            return 0

        lax.fori_loop(0, 2, side, 0)

    def multiply(ph):
        acc[...] = jnp.zeros_like(acc)
        first = min(2, groups - 1)
        for d in range(1, groups):
            relay(ph, d)
            if d == first:
                for j in range(ncb):
                    columns_in(ph, j)

                def early(e, _):
                    compute(ph, e)
                    return 0

                lax.fori_loop(0, first + 1, early, 0)
            elif d > first:
                compute(ph, d)

    def block(i, j):
        return pl.ds(i * bdim, bdim), pl.ds(j * bdim, bdim)

    def trace_of(ref_value):
        total = jnp.zeros((bdim, bdim), F32)
        eye = lax.broadcasted_iota(jnp.int32, (bdim, bdim), 0) == lax.broadcasted_iota(
            jnp.int32, (bdim, bdim), 1
        )
        for i in range(nrb):
            for j in range(ncb):
                hit = r * nrb + i == c * ncb + j
                total += jnp.where(eye & hit, ref_value(i, j), 0.0)
        return jnp.sum(total, axis=0, keepdims=True)

    for j in range(ncb):
        for i in range(nrb):
            value = dens[block(i, j)] * meta[at["occupied"] + i * ncb + j].astype(F32).astype(BF16)
            panel[0][c, j, pl.ds(i * bdim, bdim), :] = value
            column[0][j][r, i] = value
        own_col(0, j, start)
        own_row(0, j, start)
    pat_row[c] = pat[...]
    pat_col[r] = pat[...]
    for d in range(1, nrow):
        small_row(pat_col, pc_send, pc_recv, r, d).start()
    for d in range(1, ncol):
        small_col(pat_row, pr_send, pr_recv, c, d).start()

    multiply(0)
    for j in range(ncb):
        for i in range(nrb):
            keep = meta[at["keep"] + i * ncb + j].astype(F32)
            value = (acc[block(i, j)] * keep).astype(BF16)
            panel[1][c, j, pl.ds(i * bdim, bdim), :] = value
            column[1][j][r, i] = value
        own_row(1, j, start)
        own_col(1, j, start)
    diag[...] = jnp.zeros_like(diag)
    diag[0:1, :] = trace_of(lambda i, j: panel[1][c, j, pl.ds(i * bdim, bdim), :].astype(F32))

    for d in range(1, ncol):
        small_col(pat_row, pr_send, pr_recv, other_col(d), 1).wait_recv()
    for d in range(1, nrow):
        small_row(pat_col, pc_send, pc_recv, other_row(d), 1).wait_recv()
    for j in range(ncb):
        relayed(1, 1, j, start, True)
        columns_in(1, j)
        for i in range(nrb):
            mask = pat_row[
                meta[at["col_to_dev"] + j], meta[at["col_to_local"] + j] * nrb + i
            ].astype(BF16)
            value = column[1][j][meta[at["row_dev"] + i], meta[at["row_local"] + i]]
            panel[2][c, j, pl.ds(i * bdim, bdim), :] = value * mask
        own_col(2, j, start)
    for d in range(2, groups):
        relay(1, d)

    @pl.when(inner)
    def _():
        def arrived(k, _):
            from_partner(1, k)
            return 0

        lax.fori_loop(0, groups, arrived, 0)

        @pl.when((g == groups - 2) | (g == 1))
        def _():
            for j in range(ncb):
                served[j] = panel[1][meta[at["serve_dev"] + j], meta[at["serve_local"] + j]]
                serve(j, start)

        for j in range(ncb):
            given[j] = panel[1][meta[at["col_dev"] + j], meta[at["col_local"] + j]]

    @pl.when(jnp.logical_not(inner))
    def _():
        for j in range(ncb):
            give(j, partner).wait_recv()

    for j in range(ncb):
        for i in range(nrb):
            mask = pat_col[
                meta[at["row_to_dev"] + i], meta[at["row_to_local"] + i] + nrb * j
            ].astype(BF16)
            value = given[j, pl.ds(i * bdim, bdim), :]
            column[2][j][r, i] = value * mask
        own_row(2, j, start)
    multiply(2)
    for j in range(ncb):
        for i in range(nrb):
            keep = meta[at["keep"] + (nrb + i) * ncb + j].astype(F32)
            operand = panel[2][meta[at["col_dev"] + j], meta[at["col_local"] + j], pl.ds(i * bdim, bdim), :
            ]
            out[block(i, j)] = ((2.0 * operand.astype(F32) - acc[block(i, j)]) * keep).astype(BF16)
    diag[1:2, :] = trace_of(lambda i, j: out[block(i, j)].astype(F32))

    sum_row[r] = diag[...]
    for d in range(1, nrow):
        small_row(sum_row, sr_send, sr_recv, r, d).start()
    for ph in range(3):
        finish(ph)

    @pl.when((g == groups - 2) | (g == 1))
    def _():
        for j in range(ncb):
            serve(j, sent)

    for d in range(1, nrow):
        small_row(sum_row, sr_send, sr_recv, other_row(d), 1).wait_recv()
    sum_col[c] = functools.reduce(lambda a, b: a + b, [sum_row[k] for k in range(nrow)])
    for d in range(1, ncol):
        small_col(sum_col, sc_send, sc_recv, c, d).start()
    for d in range(1, ncol):
        small_col(sum_col, sc_send, sc_recv, other_col(d), 1).wait_recv()
    total = functools.reduce(lambda a, b: a + b, [sum_col[k] for k in range(ncol)])
    traces[...] = jnp.broadcast_to(jnp.sum(total, axis=1, keepdims=True), traces.shape)
    for d in range(1, nrow):
        small_row(pat_col, pc_send, pc_recv, r, d).wait_send()
        small_row(sum_row, sr_send, sr_recv, r, d).wait_send()
    for d in range(1, ncol):
        small_col(pat_row, pr_send, pr_recv, c, d).wait_send()
        small_col(sum_col, sc_send, sc_recv, c, d).wait_send()


def body(density, pattern, kept_slots, owner_shift, owner_slot):
    rows, cols = density.shape
    nrb, ncb = pattern.shape[1:]
    nrow, ncol = lax.axis_size("row"), lax.axis_size("col")
    nblocks = nrow * nrb
    row_index, col_index = lax.axis_index("row"), lax.axis_index("col")

    blocks = jnp.arange(nblocks, dtype=jnp.int32)
    shift = jnp.tile(owner_shift, nrow)
    group_to = (blocks // nrb + shift) % nrow
    local = jnp.tile(jnp.arange(nrb, dtype=jnp.int32), nrow)
    slot_hit = (group_to[:, None, None] == jnp.arange(nrow)[None, :, None]) & (
        local[:, None, None] == jnp.arange(nrb)[None, None, :]
    )
    target = group_to * nrb + jnp.sum(jnp.where(slot_hit, owner_slot[None], 0), axis=(1, 2))
    row_blocks = row_index * nrb + jnp.arange(nrb, dtype=jnp.int32)
    col_blocks = col_index * ncb + jnp.arange(ncb, dtype=jnp.int32)

    def source_of(wanted):
        return jnp.sum(jnp.where(wanted[:, None] == target[None, :], blocks[None, :], 0), axis=1)

    source_rows, source_cols = source_of(row_blocks), source_of(col_blocks)
    serve_col = jnp.where(col_index // 2 == 1, col_index - 2, lax.rem(col_index + 2, ncol))
    served_cols = source_of(serve_col * ncb + jnp.arange(ncb, dtype=jnp.int32))
    target_rows = lax.dynamic_slice(target, (row_index * nrb,), (nrb,))
    target_cols = lax.dynamic_slice(target, (col_index * ncb,), (ncb,))
    slots = jnp.arange(nrb * ncb, dtype=jnp.int32)
    keep = jnp.any(kept_slots[:, 0, 0, :, None] == slots, axis=1)
    fields = {
        "row_dev": source_rows // nrb,
        "row_local": source_rows % nrb,
        "col_dev": source_cols // ncb,
        "col_local": source_cols % ncb,
        "serve_dev": served_cols // ncb,
        "serve_local": served_cols % ncb,
        "row_to_dev": target_rows // nrb,
        "row_to_local": target_rows % nrb,
        "col_to_dev": target_cols // ncb,
        "col_to_local": target_cols % ncb,
        "occupied": pattern[0].reshape(-1),
        "keep": keep.reshape(-1).astype(jnp.int32),
    }
    at, offset = {}, 0
    for name, value in fields.items():
        at[name] = offset
        offset += value.size
    meta = jnp.concatenate([value.astype(jnp.int32) for value in fields.values()])
    small = jnp.broadcast_to(pattern[1].T.astype(F32).reshape(ncb * nrb, 1, 1), (ncb * nrb, 1, 128))

    dma = pltpu.SemaphoreType.DMA
    vmem = pl.BlockSpec(memory_space=pltpu.VMEM)
    scratch = [
        *[pltpu.VMEM((ncol, ncb, rows, rows // nrb), BF16)] * 3,
        *[pltpu.VMEM((nrow, nrb, rows // nrb, rows // nrb), BF16)] * (3 * ncb),
        pltpu.VMEM((ncol, ncb * nrb, 1, 128), F32),
        pltpu.VMEM((nrow, ncb * nrb, 1, 128), F32),
        pltpu.VMEM((nrow, 8, 128), F32),
        pltpu.VMEM((ncol, 8, 128), F32),
        pltpu.VMEM((rows, cols), F32),
        pltpu.VMEM((8, 128), F32),
        *[pltpu.VMEM((ncb, rows, rows // nrb), BF16)] * 2,
    ]
    held = 3 * (nrow + ncol) * rows * cols * 2
    second, sums = pl.pallas_call(
        functools.partial(kernel, nrow, ncol, nrb, ncb, at),
        out_shape=(
            jax.ShapeDtypeStruct((rows, cols), BF16),
            jax.ShapeDtypeStruct((8, 128), F32),
        ),
        in_specs=[pl.BlockSpec(memory_space=pltpu.SMEM), vmem, vmem],
        out_specs=(vmem, vmem),
        scratch_shapes=scratch
        + [dma((3, ncol, ncb))] * 4
        + [dma((3, nrow, ncb))] * 2
        + [dma((ncol,))] * 2
        + [dma((nrow,))] * 4
        + [dma((ncol,))] * 2
        + [dma((ncb,))] * 2,
        compiler_params=pltpu.CompilerParams(
            collective_id=0, has_side_effects=True, vmem_limit_bytes=held + (10 << 20)
        ),
        cost_estimate=pl.CostEstimate(
            flops=4 * rows * cols * nblocks * rows // nrb,
            bytes_accessed=4 * rows * cols,
            transcendentals=0,
        ),
    )(meta, density, small)
    return second, sums[:2, 0]


def solution(mesh):
    placed = (P("row", "col"), P(None, "row", "col"), P(None, "row", "col", None), P(), P())
    return jax.shard_map(
        body, mesh=mesh, in_specs=placed, out_specs=(P("row", "col"), P()), check_vma=False
    )
```

```python
import functools

import jax
import jax.numpy as jnp
from jax import lax
from jax.experimental import pallas as pl
from jax.experimental.pallas import tpu as pltpu
from jax.sharding import PartitionSpec as P

MESH = pl.DeviceIdType.MESH
F32 = jnp.float32
BF16 = jnp.bfloat16


def kernel(
    nrow, ncol, nrb, ncb, at,
    meta, dens, pat, out, traces,
    panel_0, panel_1, panel_2, *rest,
):
    panel = (panel_0, panel_1, panel_2)
    column = [rest[ph * ncb : (ph + 1) * ncb] for ph in range(3)]
    (
        pat_row, pat_col, sum_row, sum_col, acc, diag, served, given,
        p_recv, p_up, p_down, p_part, c_recv, c_send,
        pr_recv, pr_send, pc_recv, pc_send, sr_recv, sr_send, sc_recv, sc_send,
        give_recv, give_send,
    ) = rest[3 * ncb :]
    rows, cols = dens.shape
    bdim = rows // nrb
    groups = ncol // 2
    r, c = lax.axis_index("row"), lax.axis_index("col")
    g, parity = c // 2, c % 2
    partner = 2 * g + 1 - parity

    def other_row(d):
        return lax.rem(r + d, nrow)

    def other_col(d):
        return lax.rem(c + d, ncol)

    barrier = pltpu.get_barrier_semaphore()
    for d in range(1, nrow):
        pl.semaphore_signal(barrier, inc=1, device_id=(other_row(d), c), device_id_type=MESH)
    for d in range(1, ncol):
        pl.semaphore_signal(barrier, inc=1, device_id=(r, other_col(d)), device_id_type=MESH)
    pl.semaphore_wait(barrier, nrow + ncol - 2)

    def remote(ref, send, recv, device):
        return pltpu.make_async_remote_copy(
            src_ref=ref, dst_ref=ref, send_sem=send, recv_sem=recv,
            device_id=device, device_id_type=MESH,
        )

    def along_col(ph, slot, j, to, sem):
        return remote(panel[ph].at[slot, j], sem.at[ph, slot, j], p_recv.at[ph, slot, j], (r, to))

    def along_row(ph, slot, j, to, d):
        return remote(column[ph][j].at[slot], c_send.at[ph, d, j], c_recv.at[ph, slot, j], (to, c))

    def small_row(buf, send, recv, slot, d):
        return remote(buf.at[slot], send.at[d], recv.at[slot], (other_row(d), c))

    def small_col(buf, send, recv, slot, d):
        return remote(buf.at[slot], send.at[d], recv.at[slot], (r, other_col(d)))

    inner = (g > 0) & (g + 1 < groups)

    def lanes(ph):
        end = 1 if ph == 1 else 0
        return g + 1 < groups - end, g > end, inner if ph == 1 else g >= 0

    def hand_on(ph, slot, j, up, down, act):
        if up is not None:
            @pl.when(up)
            def _():
                act(along_col(ph, slot, j, c + 2, p_up))

        if down is not None:
            @pl.when(down)
            def _():
                act(along_col(ph, slot, j, c - 2, p_down))

    def start(copy):
        copy.start()

    def sent(copy):
        copy.wait_send()

    def own_col(ph, j, act):
        up, down, any_in = lanes(ph)
        hand_on(ph, c, j, up, down, act)

        @pl.when(any_in)
        def _():
            act(along_col(ph, c, j, partner, p_part))

    def own_row(ph, j, act):
        for d in range(1, nrow):
            act(along_row(ph, r, j, other_row(d), d))

    def relayed(ph, d, j, act, incoming):
        up, down, any_in = lanes(ph)
        for group, inside, to_up, to_down in (
            (g - d, g - d >= 0, up, None),
            (g + d, g + d < groups, None, down),
        ):
            @pl.when(inside & any_in)
            def _():
                slot = 2 * group + parity
                if incoming:
                    along_col(ph, slot, j, partner, p_part).wait_recv()
                hand_on(ph, slot, j, to_up, to_down, act)
                act(along_col(ph, slot, j, partner, p_part))

    def relay(ph, d):
        for j in range(ncb):
            relayed(ph, d, j, start, True)

    def from_partner(ph, group):
        for j in range(ncb):
            along_col(ph, 2 * group + 1 - parity, j, partner, p_part).wait_recv()

    def columns_in(ph, j):
        for d in range(1, nrow):
            along_row(ph, other_row(d), j, other_row(1), d).wait_recv()

    def finish(ph):
        for j in range(ncb):
            own_col(ph, j, sent)
            own_row(ph, j, sent)
            for d in range(1, groups):
                relayed(ph, d, j, sent, False)

    def serve(j, act):
        @pl.when(g == groups - 2)
        def _():
            act(give(j, c + 2))

        @pl.when(g == 1)
        def _():
            act(give(j, c - 2))

    def give(j, to):
        return pltpu.make_async_remote_copy(
            src_ref=served.at[j], dst_ref=given.at[j],
            send_sem=give_send.at[j], recv_sem=give_recv.at[j],
            device_id=(r, to), device_id_type=MESH,
        )

    half = rows // 2

    def compute(ph, d):
        def side(s, _):
            group = g + (2 * s - 1) * d

            @pl.when((group >= 0) & (group < groups) & ((d > 0) | (s > 0)))
            def _():
                from_partner(ph, group)

                def part(q, _):
                    right = jnp.concatenate(
                        [column[ph][j][group, pl.ds(q * ncb, ncb)].reshape(cols, bdim) for j in range(ncb)],
                        axis=1,
                    )
                    for k in range(2):
                        here = pl.ds(k * half, half)
                        left = jnp.concatenate(
                            [panel[ph][2 * group + q, j, here, :] for j in range(ncb)], axis=1
                        )
                        acc[here, :] += jnp.dot(left, right, preferred_element_type=F32)
                    return 0

                lax.fori_loop(0, 2, part, 0)

            return 0

        lax.fori_loop(0, 2, side, 0)

    def multiply(ph):
        acc[...] = jnp.zeros_like(acc)
        first = min(2, groups - 1)
        for d in range(1, groups):
            relay(ph, d)
            if d == first:
                for j in range(ncb):
                    columns_in(ph, j)

                def early(e, _):
                    compute(ph, e)
                    return 0

                lax.fori_loop(0, first + 1, early, 0)
            elif d > first:
                compute(ph, d)

    def block(i, j):
        return pl.ds(i * bdim, bdim), pl.ds(j * bdim, bdim)

    def trace_of(ref_value):
        total = jnp.zeros((bdim, bdim), F32)
        eye = lax.broadcasted_iota(jnp.int32, (bdim, bdim), 0) == lax.broadcasted_iota(
            jnp.int32, (bdim, bdim), 1
        )
        for i in range(nrb):
            for j in range(ncb):
                hit = r * nrb + i == c * ncb + j
                total += jnp.where(eye & hit, ref_value(i, j), 0.0)
        return jnp.sum(total, axis=0, keepdims=True)

    for j in range(ncb):
        for i in range(nrb):
            value = dens[block(i, j)] * meta[at["occupied"] + i * ncb + j].astype(F32).astype(BF16)
            panel[0][c, j, pl.ds(i * bdim, bdim), :] = value
            column[0][j][r, i] = value
        own_col(0, j, start)
        own_row(0, j, start)
    pat_row[c] = pat[...]
    pat_col[r] = pat[...]
    for d in range(1, nrow):
        small_row(pat_col, pc_send, pc_recv, r, d).start()
    for d in range(1, ncol):
        small_col(pat_row, pr_send, pr_recv, c, d).start()

    multiply(0)
    for j in range(ncb):
        for i in range(nrb):
            keep = meta[at["keep"] + i * ncb + j].astype(F32)
            value = (acc[block(i, j)] * keep).astype(BF16)
            panel[1][c, j, pl.ds(i * bdim, bdim), :] = value
            column[1][j][r, i] = value
        own_row(1, j, start)
        own_col(1, j, start)
    diag[...] = jnp.zeros_like(diag)
    diag[0:1, :] = trace_of(lambda i, j: panel[1][c, j, pl.ds(i * bdim, bdim), :].astype(F32))

    for d in range(1, ncol):
        small_col(pat_row, pr_send, pr_recv, other_col(d), 1).wait_recv()
    for d in range(1, nrow):
        small_row(pat_col, pc_send, pc_recv, other_row(d), 1).wait_recv()
    relay(1, 1)
    for j in range(ncb):
        columns_in(1, j)
        for i in range(nrb):
            mask = pat_row[
                meta[at["col_to_dev"] + j], meta[at["col_to_local"] + j] * nrb + i
            ].astype(BF16)
            value = column[1][j][meta[at["row_dev"] + i], meta[at["row_local"] + i]]
            panel[2][c, j, pl.ds(i * bdim, bdim), :] = value * mask
        own_col(2, j, start)
    for d in range(2, groups):
        relay(1, d)

    @pl.when(inner)
    def _():
        def arrived(k, _):
            from_partner(1, k)
            return 0

        lax.fori_loop(0, groups, arrived, 0)

        @pl.when((g == groups - 2) | (g == 1))
        def _():
            for j in range(ncb):
                served[j] = panel[1][meta[at["serve_dev"] + j], meta[at["serve_local"] + j]]
                serve(j, start)

        for j in range(ncb):
            given[j] = panel[1][meta[at["col_dev"] + j], meta[at["col_local"] + j]]

    @pl.when(jnp.logical_not(inner))
    def _():
        for j in range(ncb):
            give(j, partner).wait_recv()

    for j in range(ncb):
        for i in range(nrb):
            mask = pat_col[
                meta[at["row_to_dev"] + i], meta[at["row_to_local"] + i] + nrb * j
            ].astype(BF16)
            value = given[j, pl.ds(i * bdim, bdim), :]
            column[2][j][r, i] = value * mask
        own_row(2, j, start)
    multiply(2)
    for j in range(ncb):
        for i in range(nrb):
            keep = meta[at["keep"] + (nrb + i) * ncb + j].astype(F32)
            operand = panel[2][meta[at["col_dev"] + j], meta[at["col_local"] + j], pl.ds(i * bdim, bdim), :
            ]
            out[block(i, j)] = ((2.0 * operand.astype(F32) - acc[block(i, j)]) * keep).astype(BF16)
    diag[1:2, :] = trace_of(lambda i, j: out[block(i, j)].astype(F32))

    sum_row[r] = diag[...]
    for d in range(1, nrow):
        small_row(sum_row, sr_send, sr_recv, r, d).start()
    for ph in range(3):
        finish(ph)

    @pl.when((g == groups - 2) | (g == 1))
    def _():
        for j in range(ncb):
            serve(j, sent)

    for d in range(1, nrow):
        small_row(sum_row, sr_send, sr_recv, other_row(d), 1).wait_recv()
    sum_col[c] = functools.reduce(lambda a, b: a + b, [sum_row[k] for k in range(nrow)])
    for d in range(1, ncol):
        small_col(sum_col, sc_send, sc_recv, c, d).start()
    for d in range(1, ncol):
        small_col(sum_col, sc_send, sc_recv, other_col(d), 1).wait_recv()
    total = functools.reduce(lambda a, b: a + b, [sum_col[k] for k in range(ncol)])
    traces[...] = jnp.broadcast_to(jnp.sum(total, axis=1, keepdims=True), traces.shape)
    for d in range(1, nrow):
        small_row(pat_col, pc_send, pc_recv, r, d).wait_send()
        small_row(sum_row, sr_send, sr_recv, r, d).wait_send()
    for d in range(1, ncol):
        small_col(pat_row, pr_send, pr_recv, c, d).wait_send()
        small_col(sum_col, sc_send, sc_recv, c, d).wait_send()


def body(density, pattern, kept_slots, owner_shift, owner_slot):
    rows, cols = density.shape
    nrb, ncb = pattern.shape[1:]
    nrow, ncol = lax.axis_size("row"), lax.axis_size("col")
    nblocks = nrow * nrb
    row_index, col_index = lax.axis_index("row"), lax.axis_index("col")

    blocks = jnp.arange(nblocks, dtype=jnp.int32)
    shift = jnp.tile(owner_shift, nrow)
    group_to = (blocks // nrb + shift) % nrow
    local = jnp.tile(jnp.arange(nrb, dtype=jnp.int32), nrow)
    slot_hit = (group_to[:, None, None] == jnp.arange(nrow)[None, :, None]) & (
        local[:, None, None] == jnp.arange(nrb)[None, None, :]
    )
    target = group_to * nrb + jnp.sum(jnp.where(slot_hit, owner_slot[None], 0), axis=(1, 2))
    row_blocks = row_index * nrb + jnp.arange(nrb, dtype=jnp.int32)
    col_blocks = col_index * ncb + jnp.arange(ncb, dtype=jnp.int32)

    def source_of(wanted):
        return jnp.sum(jnp.where(wanted[:, None] == target[None, :], blocks[None, :], 0), axis=1)

    source_rows, source_cols = source_of(row_blocks), source_of(col_blocks)
    serve_col = jnp.where(col_index // 2 == 1, col_index - 2, lax.rem(col_index + 2, ncol))
    served_cols = source_of(serve_col * ncb + jnp.arange(ncb, dtype=jnp.int32))
    target_rows = lax.dynamic_slice(target, (row_index * nrb,), (nrb,))
    target_cols = lax.dynamic_slice(target, (col_index * ncb,), (ncb,))
    slots = jnp.arange(nrb * ncb, dtype=jnp.int32)
    keep = jnp.any(kept_slots[:, 0, 0, :, None] == slots, axis=1)
    fields = {
        "row_dev": source_rows // nrb,
        "row_local": source_rows % nrb,
        "col_dev": source_cols // ncb,
        "col_local": source_cols % ncb,
        "serve_dev": served_cols // ncb,
        "serve_local": served_cols % ncb,
        "row_to_dev": target_rows // nrb,
        "row_to_local": target_rows % nrb,
        "col_to_dev": target_cols // ncb,
        "col_to_local": target_cols % ncb,
        "occupied": pattern[0].reshape(-1),
        "keep": keep.reshape(-1).astype(jnp.int32),
    }
    at, offset = {}, 0
    for name, value in fields.items():
        at[name] = offset
        offset += value.size
    meta = jnp.concatenate([value.astype(jnp.int32) for value in fields.values()])
    small = jnp.broadcast_to(pattern[1].T.astype(F32).reshape(ncb * nrb, 1, 1), (ncb * nrb, 1, 128))

    dma = pltpu.SemaphoreType.DMA
    vmem = pl.BlockSpec(memory_space=pltpu.VMEM)
    scratch = [
        *[pltpu.VMEM((ncol, ncb, rows, rows // nrb), BF16)] * 3,
        *[pltpu.VMEM((nrow, nrb, rows // nrb, rows // nrb), BF16)] * (3 * ncb),
        pltpu.VMEM((ncol, ncb * nrb, 1, 128), F32),
        pltpu.VMEM((nrow, ncb * nrb, 1, 128), F32),
        pltpu.VMEM((nrow, 8, 128), F32),
        pltpu.VMEM((ncol, 8, 128), F32),
        pltpu.VMEM((rows, cols), F32),
        pltpu.VMEM((8, 128), F32),
        *[pltpu.VMEM((ncb, rows, rows // nrb), BF16)] * 2,
    ]
    held = 3 * (nrow + ncol) * rows * cols * 2
    second, sums = pl.pallas_call(
        functools.partial(kernel, nrow, ncol, nrb, ncb, at),
        out_shape=(
            jax.ShapeDtypeStruct((rows, cols), BF16),
            jax.ShapeDtypeStruct((8, 128), F32),
        ),
        in_specs=[pl.BlockSpec(memory_space=pltpu.SMEM), vmem, vmem],
        out_specs=(vmem, vmem),
        scratch_shapes=scratch
        + [dma((3, ncol, ncb))] * 4
        + [dma((3, nrow, ncb))] * 2
        + [dma((ncol,))] * 2
        + [dma((nrow,))] * 4
        + [dma((ncol,))] * 2
        + [dma((ncb,))] * 2,
        compiler_params=pltpu.CompilerParams(
            collective_id=0, has_side_effects=True, vmem_limit_bytes=held + (10 << 20)
        ),
        cost_estimate=pl.CostEstimate(
            flops=4 * rows * cols * nblocks * rows // nrb,
            bytes_accessed=4 * rows * cols,
            transcendentals=0,
        ),
    )(meta, density, small)
    return second, sums[:2, 0]


def solution(mesh):
    placed = (P("row", "col"), P(None, "row", "col"), P(None, "row", "col", None), P(), P())
    return jax.shard_map(
        body, mesh=mesh, in_specs=placed, out_specs=(P("row", "col"), P()), check_vma=False
    )
```

```python
import functools

import jax
import jax.numpy as jnp
from jax import lax
from jax.experimental import pallas as pl
from jax.experimental.pallas import tpu as pltpu
from jax.sharding import PartitionSpec as P

MESH = pl.DeviceIdType.MESH
F32 = jnp.float32
BF16 = jnp.bfloat16


def kernel(
    nrow, ncol, nrb, ncb, at,
    meta, dens, pat, out, traces,
    panel_0, panel_1, panel_2, *rest,
):
    panel = (panel_0, panel_1, panel_2)
    column = [rest[ph * ncb : (ph + 1) * ncb] for ph in range(3)]
    (
        pat_row, pat_col, sum_row, sum_col, acc, diag, served, given,
        p_recv, p_up, p_down, p_part, c_recv, c_send,
        pr_recv, pr_send, pc_recv, pc_send, sr_recv, sr_send, sc_recv, sc_send,
        give_recv, give_send,
    ) = rest[3 * ncb :]
    rows, cols = dens.shape
    bdim = rows // nrb
    groups = ncol // 2
    r, c = lax.axis_index("row"), lax.axis_index("col")
    g, parity = c // 2, c % 2
    partner = 2 * g + 1 - parity

    def other_row(d):
        return lax.rem(r + d, nrow)

    def other_col(d):
        return lax.rem(c + d, ncol)

    barrier = pltpu.get_barrier_semaphore()
    for d in range(1, nrow):
        pl.semaphore_signal(barrier, inc=1, device_id=(other_row(d), c), device_id_type=MESH)
    for d in range(1, ncol):
        pl.semaphore_signal(barrier, inc=1, device_id=(r, other_col(d)), device_id_type=MESH)
    pl.semaphore_wait(barrier, nrow + ncol - 2)

    def remote(ref, send, recv, device):
        return pltpu.make_async_remote_copy(
            src_ref=ref, dst_ref=ref, send_sem=send, recv_sem=recv,
            device_id=device, device_id_type=MESH,
        )

    def along_col(ph, slot, j, to, sem):
        return remote(panel[ph].at[slot, j], sem.at[ph, slot, j], p_recv.at[ph, slot, j], (r, to))

    def along_row(ph, slot, j, to, d):
        return remote(column[ph][j].at[slot], c_send.at[ph, d, j], c_recv.at[ph, slot, j], (to, c))

    def small_row(buf, send, recv, slot, d):
        return remote(buf.at[slot], send.at[d], recv.at[slot], (other_row(d), c))

    def small_col(buf, send, recv, slot, d):
        return remote(buf.at[slot], send.at[d], recv.at[slot], (r, other_col(d)))

    inner = (g > 0) & (g + 1 < groups)

    def lanes(ph):
        end = 1 if ph == 1 else 0
        return g + 1 < groups - end, g > end, inner if ph == 1 else g >= 0

    def hand_on(ph, slot, j, up, down, act):
        if up is not None:
            @pl.when(up)
            def _():
                act(along_col(ph, slot, j, c + 2, p_up))

        if down is not None:
            @pl.when(down)
            def _():
                act(along_col(ph, slot, j, c - 2, p_down))

    def start(copy):
        copy.start()

    def sent(copy):
        copy.wait_send()

    def own_col(ph, j, act):
        up, down, any_in = lanes(ph)
        hand_on(ph, c, j, up, down, act)

        @pl.when(any_in)
        def _():
            act(along_col(ph, c, j, partner, p_part))

    def own_row(ph, j, act):
        for d in range(1, nrow):
            act(along_row(ph, r, j, other_row(d), d))

    def relayed(ph, d, j, act, incoming):
        up, down, any_in = lanes(ph)
        for group, inside, to_up, to_down in (
            (g - d, g - d >= 0, up, None),
            (g + d, g + d < groups, None, down),
        ):
            @pl.when(inside & any_in)
            def _():
                slot = 2 * group + parity
                if incoming:
                    along_col(ph, slot, j, partner, p_part).wait_recv()
                hand_on(ph, slot, j, to_up, to_down, act)
                act(along_col(ph, slot, j, partner, p_part))

    def relay(ph, d):
        for j in range(ncb):
            relayed(ph, d, j, start, True)

    def from_partner(ph, group):
        for j in range(ncb):
            along_col(ph, 2 * group + 1 - parity, j, partner, p_part).wait_recv()

    def columns_in(ph, j):
        for d in range(1, nrow):
            along_row(ph, other_row(d), j, other_row(1), d).wait_recv()

    def finish(ph):
        for j in range(ncb):
            own_col(ph, j, sent)
            own_row(ph, j, sent)
            for d in range(1, groups):
                relayed(ph, d, j, sent, False)

    def serve(j, act):
        @pl.when(g == groups - 2)
        def _():
            act(give(j, c + 2))

        @pl.when(g == 1)
        def _():
            act(give(j, c - 2))

    def give(j, to):
        return pltpu.make_async_remote_copy(
            src_ref=served.at[j], dst_ref=given.at[j],
            send_sem=give_send.at[j], recv_sem=give_recv.at[j],
            device_id=(r, to), device_id_type=MESH,
        )

    half = rows // 2

    def compute(ph, d):
        def side(s, _):
            group = g + (2 * s - 1) * d

            @pl.when((group >= 0) & (group < groups) & ((d > 0) | (s > 0)))
            def _():
                from_partner(ph, group)

                def part(q, _):
                    right = jnp.concatenate(
                        [column[ph][j][group, pl.ds(q * ncb, ncb)].reshape(cols, bdim) for j in range(ncb)],
                        axis=1,
                    )
                    for k in range(2):
                        here = pl.ds(k * half, half)
                        left = jnp.concatenate(
                            [panel[ph][2 * group + q, j, here, :] for j in range(ncb)], axis=1
                        )
                        acc[here, :] += jnp.dot(left, right, preferred_element_type=F32)
                    return 0

                lax.fori_loop(0, 2, part, 0)

            return 0

        lax.fori_loop(0, 2, side, 0)

    def multiply(ph):
        acc[...] = jnp.zeros_like(acc)
        first = min(2, groups - 1)
        for d in range(1, groups):
            relay(ph, d)
            if d == first:
                for j in range(ncb):
                    columns_in(ph, j)

                def early(e, _):
                    compute(ph, e)
                    return 0

                lax.fori_loop(0, first + 1, early, 0)
            elif d > first:
                compute(ph, d)

    def block(i, j):
        return pl.ds(i * bdim, bdim), pl.ds(j * bdim, bdim)

    def trace_of(ref_value):
        total = jnp.zeros((bdim, bdim), F32)
        eye = lax.broadcasted_iota(jnp.int32, (bdim, bdim), 0) == lax.broadcasted_iota(
            jnp.int32, (bdim, bdim), 1
        )
        for i in range(nrb):
            for j in range(ncb):
                hit = r * nrb + i == c * ncb + j
                total += jnp.where(eye & hit, ref_value(i, j), 0.0)
        return jnp.sum(total, axis=0, keepdims=True)

    for j in range(ncb):
        for i in range(nrb):
            value = dens[block(i, j)] * meta[at["occupied"] + i * ncb + j].astype(F32).astype(BF16)
            panel[0][c, j, pl.ds(i * bdim, bdim), :] = value
            column[0][j][r, i] = value
        own_col(0, j, start)
        own_row(0, j, start)
    pat_row[c] = pat[...]
    pat_col[r] = pat[...]
    for d in range(1, nrow):
        small_row(pat_col, pc_send, pc_recv, r, d).start()
    for d in range(1, ncol):
        small_col(pat_row, pr_send, pr_recv, c, d).start()

    multiply(0)
    for j in range(ncb):
        for i in range(nrb):
            keep = meta[at["keep"] + i * ncb + j].astype(F32)
            value = (acc[block(i, j)] * keep).astype(BF16)
            panel[1][c, j, pl.ds(i * bdim, bdim), :] = value
            column[1][j][r, i] = value
        if j + 1 < ncb:
            own_row(1, j, start)
        own_col(1, j, start)
    diag[...] = jnp.zeros_like(diag)
    diag[0:1, :] = trace_of(lambda i, j: panel[1][c, j, pl.ds(i * bdim, bdim), :].astype(F32))

    for d in range(1, ncol):
        small_col(pat_row, pr_send, pr_recv, other_col(d), 1).wait_recv()
    for d in range(1, nrow):
        small_row(pat_col, pc_send, pc_recv, other_row(d), 1).wait_recv()
    relay(1, 1)
    own_row(1, ncb - 1, start)
    for j in range(ncb):
        columns_in(1, j)
        for i in range(nrb):
            mask = pat_row[
                meta[at["col_to_dev"] + j], meta[at["col_to_local"] + j] * nrb + i
            ].astype(BF16)
            value = column[1][j][meta[at["row_dev"] + i], meta[at["row_local"] + i]]
            panel[2][c, j, pl.ds(i * bdim, bdim), :] = value * mask
        own_col(2, j, start)
    for d in range(2, groups):
        relay(1, d)

    @pl.when(inner)
    def _():
        def arrived(k, _):
            from_partner(1, k)
            return 0

        lax.fori_loop(0, groups, arrived, 0)

        @pl.when((g == groups - 2) | (g == 1))
        def _():
            for j in range(ncb):
                served[j] = panel[1][meta[at["serve_dev"] + j], meta[at["serve_local"] + j]]
                serve(j, start)

        for j in range(ncb):
            given[j] = panel[1][meta[at["col_dev"] + j], meta[at["col_local"] + j]]

    @pl.when(jnp.logical_not(inner))
    def _():
        for j in range(ncb):
            give(j, partner).wait_recv()

    for j in range(ncb):
        for i in range(nrb):
            mask = pat_col[
                meta[at["row_to_dev"] + i], meta[at["row_to_local"] + i] + nrb * j
            ].astype(BF16)
            value = given[j, pl.ds(i * bdim, bdim), :]
            column[2][j][r, i] = value * mask
        own_row(2, j, start)
    multiply(2)
    for j in range(ncb):
        for i in range(nrb):
            keep = meta[at["keep"] + (nrb + i) * ncb + j].astype(F32)
            operand = panel[2][meta[at["col_dev"] + j], meta[at["col_local"] + j], pl.ds(i * bdim, bdim), :
            ]
            out[block(i, j)] = ((2.0 * operand.astype(F32) - acc[block(i, j)]) * keep).astype(BF16)
    diag[1:2, :] = trace_of(lambda i, j: out[block(i, j)].astype(F32))

    sum_row[r] = diag[...]
    for d in range(1, nrow):
        small_row(sum_row, sr_send, sr_recv, r, d).start()
    for ph in range(3):
        finish(ph)

    @pl.when((g == groups - 2) | (g == 1))
    def _():
        for j in range(ncb):
            serve(j, sent)

    for d in range(1, nrow):
        small_row(sum_row, sr_send, sr_recv, other_row(d), 1).wait_recv()
    sum_col[c] = functools.reduce(lambda a, b: a + b, [sum_row[k] for k in range(nrow)])
    for d in range(1, ncol):
        small_col(sum_col, sc_send, sc_recv, c, d).start()
    for d in range(1, ncol):
        small_col(sum_col, sc_send, sc_recv, other_col(d), 1).wait_recv()
    total = functools.reduce(lambda a, b: a + b, [sum_col[k] for k in range(ncol)])
    traces[...] = jnp.broadcast_to(jnp.sum(total, axis=1, keepdims=True), traces.shape)
    for d in range(1, nrow):
        small_row(pat_col, pc_send, pc_recv, r, d).wait_send()
        small_row(sum_row, sr_send, sr_recv, r, d).wait_send()
    for d in range(1, ncol):
        small_col(pat_row, pr_send, pr_recv, c, d).wait_send()
        small_col(sum_col, sc_send, sc_recv, c, d).wait_send()


def body(density, pattern, kept_slots, owner_shift, owner_slot):
    rows, cols = density.shape
    nrb, ncb = pattern.shape[1:]
    nrow, ncol = lax.axis_size("row"), lax.axis_size("col")
    nblocks = nrow * nrb
    row_index, col_index = lax.axis_index("row"), lax.axis_index("col")

    blocks = jnp.arange(nblocks, dtype=jnp.int32)
    shift = jnp.tile(owner_shift, nrow)
    group_to = (blocks // nrb + shift) % nrow
    local = jnp.tile(jnp.arange(nrb, dtype=jnp.int32), nrow)
    slot_hit = (group_to[:, None, None] == jnp.arange(nrow)[None, :, None]) & (
        local[:, None, None] == jnp.arange(nrb)[None, None, :]
    )
    target = group_to * nrb + jnp.sum(jnp.where(slot_hit, owner_slot[None], 0), axis=(1, 2))
    row_blocks = row_index * nrb + jnp.arange(nrb, dtype=jnp.int32)
    col_blocks = col_index * ncb + jnp.arange(ncb, dtype=jnp.int32)

    def source_of(wanted):
        return jnp.sum(jnp.where(wanted[:, None] == target[None, :], blocks[None, :], 0), axis=1)

    source_rows, source_cols = source_of(row_blocks), source_of(col_blocks)
    serve_col = jnp.where(col_index // 2 == 1, col_index - 2, lax.rem(col_index + 2, ncol))
    served_cols = source_of(serve_col * ncb + jnp.arange(ncb, dtype=jnp.int32))
    target_rows = lax.dynamic_slice(target, (row_index * nrb,), (nrb,))
    target_cols = lax.dynamic_slice(target, (col_index * ncb,), (ncb,))
    slots = jnp.arange(nrb * ncb, dtype=jnp.int32)
    keep = jnp.any(kept_slots[:, 0, 0, :, None] == slots, axis=1)
    fields = {
        "row_dev": source_rows // nrb,
        "row_local": source_rows % nrb,
        "col_dev": source_cols // ncb,
        "col_local": source_cols % ncb,
        "serve_dev": served_cols // ncb,
        "serve_local": served_cols % ncb,
        "row_to_dev": target_rows // nrb,
        "row_to_local": target_rows % nrb,
        "col_to_dev": target_cols // ncb,
        "col_to_local": target_cols % ncb,
        "occupied": pattern[0].reshape(-1),
        "keep": keep.reshape(-1).astype(jnp.int32),
    }
    at, offset = {}, 0
    for name, value in fields.items():
        at[name] = offset
        offset += value.size
    meta = jnp.concatenate([value.astype(jnp.int32) for value in fields.values()])
    small = jnp.broadcast_to(pattern[1].T.astype(F32).reshape(ncb * nrb, 1, 1), (ncb * nrb, 1, 128))

    dma = pltpu.SemaphoreType.DMA
    vmem = pl.BlockSpec(memory_space=pltpu.VMEM)
    scratch = [
        *[pltpu.VMEM((ncol, ncb, rows, rows // nrb), BF16)] * 3,
        *[pltpu.VMEM((nrow, nrb, rows // nrb, rows // nrb), BF16)] * (3 * ncb),
        pltpu.VMEM((ncol, ncb * nrb, 1, 128), F32),
        pltpu.VMEM((nrow, ncb * nrb, 1, 128), F32),
        pltpu.VMEM((nrow, 8, 128), F32),
        pltpu.VMEM((ncol, 8, 128), F32),
        pltpu.VMEM((rows, cols), F32),
        pltpu.VMEM((8, 128), F32),
        *[pltpu.VMEM((ncb, rows, rows // nrb), BF16)] * 2,
    ]
    held = 3 * (nrow + ncol) * rows * cols * 2
    second, sums = pl.pallas_call(
        functools.partial(kernel, nrow, ncol, nrb, ncb, at),
        out_shape=(
            jax.ShapeDtypeStruct((rows, cols), BF16),
            jax.ShapeDtypeStruct((8, 128), F32),
        ),
        in_specs=[pl.BlockSpec(memory_space=pltpu.SMEM), vmem, vmem],
        out_specs=(vmem, vmem),
        scratch_shapes=scratch
        + [dma((3, ncol, ncb))] * 4
        + [dma((3, nrow, ncb))] * 2
        + [dma((ncol,))] * 2
        + [dma((nrow,))] * 4
        + [dma((ncol,))] * 2
        + [dma((ncb,))] * 2,
        compiler_params=pltpu.CompilerParams(
            collective_id=0, has_side_effects=True, vmem_limit_bytes=held + (10 << 20)
        ),
        cost_estimate=pl.CostEstimate(
            flops=4 * rows * cols * nblocks * rows // nrb,
            bytes_accessed=4 * rows * cols,
            transcendentals=0,
        ),
    )(meta, density, small)
    return second, sums[:2, 0]


def solution(mesh):
    placed = (P("row", "col"), P(None, "row", "col"), P(None, "row", "col", None), P(), P())
    return jax.shard_map(
        body, mesh=mesh, in_specs=placed, out_specs=(P("row", "col"), P()), check_vma=False
    )
```
